32 devices in a mesh: groups: 2 (over x), dp: 16 (over z, y, core).
Axes of the slice: x: 2, y: 2, z: 4, core: 2. Of those that a mesh axis runs over, the one named last changes fastest.
Arguments:
- tokens: bfloat16 [4096, 8192], P(('groups', 'dp')), parts along dimension 0, may hold values from -6 to 6
- output_gradient: bfloat16 [4096, 26624], P(('groups', 'dp')), parts along dimension 0, may hold values from -0.29882812 to 0.29882812
- adapter_down_factor: bfloat16 [16, 8192, 64], P('groups', 'dp'), parts along dimension 0, may hold values from -0.0625 to 0.0625
- adapter_up_factor: bfloat16 [16, 64, 26624], P('groups', None, 'dp'), parts along dimension 0, may hold values from -0.75 to 0.75
- job_row_counts: int32 [32, 8], P(('groups', 'dp')), parts along dimension 0, may hold values from 0 to 127, as said below
Outputs:
- grad_tokens: bfloat16 [4096, 8192], P(('groups', 'dp')), parts along dimension 0
- down_grad: float32 [16, 8192, 64], P('groups', 'dp'), parts along dimension 0
- up_grad: float32 [16, 64, 26624], P('groups', None, 'dp'), parts along dimension 0
The draws below stay inside these ranges and needn't reach their ends.
There are 2 independent parts, one for each index of `groups`. The reference program is written for one: setup_inputs(seed, part) draws one part's arguments, and reference() takes and returns one part's arrays. A program takes and returns all parts, laid end to end along the dimension named above; each array names one. Nothing has to cross between parts.
Inputs may be any that keep to these rules, and one draw needn't show every extreme that they name: `job_row_counts`: every row has exactly two nonzero entries; their sum is at most 128 and equals 128 in at least one row.
All inputs are finite; a program needn't handle non-finite values.
Results may differ from the reference program's by a relative error of at most 0.008.
Values may be sent and summed in bfloat16 or wider, within the bound.
A program may use at most 128 MiB of HBM per device.

```python
import jax
import jax.numpy as jnp
from jax import lax

INPUT_FEATURES = 8192
HIDDEN_UNITS = 26624
ADAPTER_RANK = 64
ADAPTER_JOBS = 8
TOK_DEV = 128
TOKENS = 2048
N_DP = 16


def draw_job_row_counts(key, part):
    key = jax.random.fold_in(key, 11)
    key_pick, key_live, key_full, key_head = jax.random.split(key, 4)
    pick_keys = jax.random.split(key_pick, N_DP)
    picks = jax.vmap(lambda one_key: jax.random.permutation(one_key, ADAPTER_JOBS)[:2])(pick_keys)
    live_rows = jax.random.randint(key_live, (N_DP,), TOK_DEV // 2, TOK_DEV + 1)
    full_at = jax.random.randint(key_full, (), 0, N_DP)
    live_rows = jnp.where(jnp.arange(N_DP) == full_at, TOK_DEV, live_rows)
    head_rows = jax.random.randint(key_head, (N_DP,), 0, 1 << 20) % (live_rows - 1) + 1
    tail_rows = live_rows - head_rows
    leading_job = jnp.min(picks, axis=1)
    trailing_job = jnp.max(picks, axis=1)
    job_index = jnp.arange(ADAPTER_JOBS)
    counts = jnp.where(job_index[None, :] == leading_job[:, None], head_rows[:, None], 0)
    counts = counts + jnp.where(job_index[None, :] == trailing_job[:, None], tail_rows[:, None], 0)
    return counts.astype(jnp.int32)


def block_scale(rng, shape, shards, smallest, largest):
    loudness = 1.0
    for axis_at, blocks in shards:
        steps = jax.random.uniform(jax.random.fold_in(jax.random.fold_in(rng, 6), axis_at), (blocks,), jnp.float32, smallest / len(shards), largest / len(shards))
        loudness = loudness * jnp.repeat(jnp.exp(steps), shape[axis_at] // blocks).reshape((-1,) + (1,) * (len(shape) - 1 - axis_at))
    return loudness


def scatter_about(rng, shape, scale, most, cuts=(), held_as=jnp.bfloat16):
    values = scale * jax.random.normal(rng, shape, jnp.float32)
    if cuts:
        values = values * block_scale(rng, shape, cuts, -0.22, 0.18)
    return jnp.clip(values, -most, most).astype(held_as)


def setup_inputs(seed: int = 0, part: int = 0) -> dict:
    key_of = jax.random.split(jax.random.key(seed), 6)
    part_keys = jax.random.split(jax.random.fold_in(key_of[5], part), 6)
    tokens = scatter_about(part_keys[0], (TOKENS, INPUT_FEATURES), 1.0, 6.0, ((0, 16),))
    output_gradient = scatter_about(part_keys[1], (TOKENS, HIDDEN_UNITS), 0.05, 0.29882812, ((0, 16),))
    adapter_down_factor = scatter_about(part_keys[2], (ADAPTER_JOBS, INPUT_FEATURES, ADAPTER_RANK), INPUT_FEATURES ** -0.5, 0.0625, ((1, 16),))
    adapter_up_factor = scatter_about(part_keys[3], (ADAPTER_JOBS, ADAPTER_RANK, HIDDEN_UNITS), ADAPTER_RANK ** -0.5, 0.75, ((2, 16),))
    job_row_counts = draw_job_row_counts(jax.random.fold_in(jax.random.fold_in(key_of[5], part), 71), part)
    return dict(tokens=tokens, output_gradient=output_gradient, adapter_down_factor=adapter_down_factor, adapter_up_factor=adapter_up_factor, job_row_counts=job_row_counts)


ADAPTER_SCALE = 2.0


def job_pairs(counts):
    job_total = counts.shape[1]
    job_index = jnp.arange(job_total, dtype=jnp.int32)
    present = counts > 0
    leading_job = jnp.min(jnp.where(present, job_index, job_total), axis=1).astype(jnp.int32)
    trailing_job = jnp.max(jnp.where(present, job_index, -1), axis=1).astype(jnp.int32)
    head_rows = jnp.sum(jnp.where(job_index == leading_job[:, None], counts, 0), axis=1).astype(jnp.int32)
    tail_rows = jnp.sum(jnp.where(job_index == trailing_job[:, None], counts, 0), axis=1).astype(jnp.int32)
    return leading_job, trailing_job, head_rows, tail_rows


def slot_masks(head_rows, tail_rows, row_total):
    position = jnp.arange(row_total, dtype=jnp.int32)[None, :]
    first_mask = position < head_rows[:, None]
    second_mask = (position >= head_rows[:, None]) & (position < (head_rows + tail_rows)[:, None])
    return jnp.stack([first_mask, second_mask], axis=-1).astype(jnp.float32)


def reference(tokens, output_gradient, adapter_down_factor, adapter_up_factor, job_row_counts):
    block_total = job_row_counts.shape[0]
    token_blocks = tokens.reshape(block_total, TOK_DEV, INPUT_FEATURES)
    grad_blocks = output_gradient.reshape(block_total, TOK_DEV, HIDDEN_UNITS)

    def one_block(carry, item):
        down_acc, up_acc = carry
        block_tokens, block_grad, counts = item
        leading_job, trailing_job, head_rows, tail_rows = job_pairs(counts[None])
        job_masks = slot_masks(head_rows, tail_rows, TOK_DEV)[0]
        down_factor_pair = jnp.stack([adapter_down_factor[leading_job[0]], adapter_down_factor[trailing_job[0]]]).astype(jnp.float32)
        up_factor_pair = jnp.stack([adapter_up_factor[leading_job[0]], adapter_up_factor[trailing_job[0]]]).astype(jnp.float32)
        token_wide = block_tokens.astype(jnp.float32)
        gradient_broad = block_grad.astype(jnp.float32)
        code_terms = jnp.einsum("td,kdr->tkr", token_wide, down_factor_pair)
        rank_codes = jnp.sum(code_terms * job_masks[:, :, None], axis=1).astype(jnp.bfloat16)
        gradient_summands = jnp.einsum("tc,krc->tkr", gradient_broad, up_factor_pair)
        rank_gradient = (ADAPTER_SCALE * jnp.sum(gradient_summands * job_masks[:, :, None], axis=1)).astype(jnp.bfloat16)
        grad_slots = job_masks[:, :, None] * rank_gradient.astype(jnp.float32)[:, None, :]
        slot_encodings = job_masks[:, :, None] * rank_codes.astype(jnp.float32)[:, None, :]
        grad_rows = jnp.einsum("tkr,kdr->td", grad_slots, down_factor_pair).astype(jnp.bfloat16)
        down_part = jnp.einsum("td,tkr->kdr", token_wide, grad_slots)
        up_factor_portion = ADAPTER_SCALE * jnp.einsum("bpu,bi->pui", slot_encodings, gradient_broad)
        down_acc = down_acc.at[leading_job[0]].add(down_part[0]).at[trailing_job[0]].add(down_part[1])
        up_acc = up_acc.at[leading_job[0]].add(up_factor_portion[0]).at[trailing_job[0]].add(up_factor_portion[1])
        return (down_acc, up_acc), grad_rows

    start_carry = (jnp.zeros((ADAPTER_JOBS, INPUT_FEATURES, ADAPTER_RANK), jnp.float32), jnp.zeros((ADAPTER_JOBS, ADAPTER_RANK, HIDDEN_UNITS), jnp.float32))
    (down_grad, up_grad), grad_rows = lax.scan(one_block, start_carry, (token_blocks, grad_blocks, job_row_counts))
    return grad_rows.reshape(TOKENS, INPUT_FEATURES), down_grad, up_grad
```

```python
import jax
import jax.numpy as jnp
from jax import lax
from jax.sharding import PartitionSpec as P

ADAPTER_SCALE = 2.0


def row_jobs(counts, row_count):
    ends = jnp.cumsum(counts, axis=1)
    starts = ends - counts
    position = jnp.arange(row_count, dtype=jnp.int32)[None, :, None]
    hot = (position >= starts[:, None, :]) & (position < ends[:, None, :])
    return hot.reshape(counts.shape[0] * row_count, counts.shape[1])


def local(tokens, output_gradient, down_factor, up_factor, counts):
    row_count = tokens.shape[0]
    n = lax.axis_size("dp")
    jobs, _, rank = down_factor.shape
    every_count = lax.all_gather(counts, "dp", axis=0, tiled=True)
    hot = row_jobs(every_count, row_count)
    grad_cols = lax.all_to_all(output_gradient, "dp", split_axis=1, concat_axis=0, tiled=True)
    token_cols = lax.all_to_all(tokens, "dp", split_axis=1, concat_axis=0, tiled=True)

    def select(terms):
        return jnp.sum(jnp.where(hot[:, :, None], terms, 0.0), axis=1)

    code_part = select(jnp.einsum("td,jdr->tjr", token_cols, down_factor, preferred_element_type=jnp.float32))
    grad_part = select(jnp.einsum("tc,jrc->tjr", grad_cols, up_factor, preferred_element_type=jnp.float32))
    parts = jnp.concatenate([code_part, grad_part], axis=1)
    parts = lax.all_to_all(parts, "dp", split_axis=0, concat_axis=0, tiled=True)
    own = jnp.sum(parts.reshape(n, row_count, 2 * rank), axis=0)
    own = jnp.concatenate([own[:, :rank], ADAPTER_SCALE * own[:, rank:]], axis=1).astype(jnp.bfloat16)
    whole = lax.all_gather(own, "dp", axis=0, tiled=True)

    def spread(rows):
        return jnp.where(hot[:, :, None], rows[:, None, :], jnp.bfloat16(0))

    codes, grads = spread(whole[:, :rank]), spread(whole[:, rank:])
    grad_token_cols = jnp.einsum("tjr,jdr->td", grads, down_factor, preferred_element_type=jnp.float32).astype(jnp.bfloat16)
    grad_tokens = lax.all_to_all(grad_token_cols, "dp", split_axis=0, concat_axis=1, tiled=True)
    down_grad = jnp.einsum("td,tjr->jdr", token_cols, grads, preferred_element_type=jnp.float32)
    up_grad = ADAPTER_SCALE * jnp.einsum("tjr,tc->jrc", codes, grad_cols, preferred_element_type=jnp.float32)
    return grad_tokens, down_grad, up_grad


def solution(mesh):
    return jax.shard_map(
        local,
        mesh=mesh,
        in_specs=(
            P(("groups", "dp"), None),
            P(("groups", "dp"), None),
            P("groups", "dp", None),
            P("groups", None, "dp"),
            P(("groups", "dp"), None),
        ),
        out_specs=(P(("groups", "dp"), None), P("groups", "dp", None), P("groups", None, "dp")),
        check_vma=False,
    )
```

```python
import functools

import jax
import jax.numpy as jnp
from jax import lax
from jax.experimental import pallas as pl
from jax.experimental.pallas import tpu as pltpu
from jax.sharding import PartitionSpec as P

ADAPTER_SCALE = 2.0
MESH = pl.DeviceIdType.MESH
F32 = jnp.float32
BF16 = jnp.bfloat16
NN = (((1,), (0,)), ((), ()))
NT = (((1,), (1,)), ((), ()))
TN = (((0,), (0,)), ((), ()))


def dot(a, b, dims):
    return lax.dot_general(a, b, dims, preferred_element_type=F32)


def kernel(
    n, split, tok, grad, down, up, spans, gt_out, dg_out, ug_out,
    g_cols, t_cols, a_all, s_all, code_all, rank_all, part_out, part_in, acc,
    own_sem, g_s, g_r, t_s, t_r, a_s, a_r, s_s, s_r, c_s, c_r, p_s, p_r, r_s, r_r,
):
    me = lax.axis_index("dp")
    rows = tok.shape[0]
    half = rows // 2
    d_cols = t_cols.shape[2]
    c_cols = g_cols.shape[2]
    pairs = s_all.shape[1] // 2

    def push(src, dst, send, recv, to):
        return pltpu.make_async_remote_copy(
            src_ref=src, dst_ref=dst, send_sem=send, recv_sem=recv,
            device_id={"dp": to}, device_id_type=MESH,
        )

    def others(body):
        def step(k, carry):
            body(k)
            return carry
        lax.fori_loop(1, n, step, 0)

    def ahead(k):
        return lax.rem(me + k, n)

    def behind(k):
        return lax.rem(me + n - k, n)

    def grad_slice(at):
        if split:
            return grad.at[at]
        return grad.at[:, pl.ds(pl.multiple_of(at * c_cols, 128), c_cols)]

    def tok_cols(at):
        return pl.ds(pl.multiple_of(at * d_cols, 128), d_cols)

    lane = lax.broadcasted_iota(jnp.int32, (half, 128), 1)
    place = lax.broadcasted_iota(jnp.int32, (rows, 128), 0)

    def mask(block, p):
        return (place >= s_all[block, p : p + 1, :]) & (place < s_all[block, pairs + p : pairs + p + 1, :])

    def fold(block, terms):
        total = jnp.zeros((rows, 128), F32)
        for p in range(pairs):
            total += jnp.where(mask(block, p), terms[:, 128 * p : 128 * (p + 1)], 0.0)
        twice = total + pltpu.roll(total, 64, 1)
        return jnp.where(lane < 64, twice[:half], twice[half:])

    def widen(block, packed):
        x = packed.astype(F32)
        y = pltpu.roll(x, 64, 1)
        both = jnp.concatenate([jnp.where(lane < 64, x, y), jnp.where(lane < 64, y, x)], axis=0)
        return jnp.concatenate([jnp.where(mask(block, p), both, 0.0) for p in range(pairs)], axis=1).astype(BF16)

    barrier = pltpu.get_barrier_semaphore()
    others(lambda k: pl.semaphore_signal(barrier, inc=1, device_id={"dp": ahead(k)}, device_id_type=MESH))
    s_all[me] = spans[...]
    a_all[me] = down[...]
    own = pltpu.make_async_copy(grad_slice(me), g_cols.at[me], own_sem)
    own.start()
    pl.semaphore_wait(barrier, n - 1)

    def span_copy(k):
        return push(s_all.at[me], s_all.at[me], s_s.at[k], s_r.at[me], ahead(k))

    def g_copy(k):
        return push(grad_slice(ahead(k)), g_cols.at[me], g_s.at[k], g_r.at[me], ahead(k))

    def t_copy(k):
        return push(tok.at[:, tok_cols(ahead(k))], t_cols.at[me], t_s.at[k], t_r.at[me], ahead(k))

    def code_copy(k):
        return push(code_all.at[me], code_all.at[me], c_s.at[k], c_r.at[me], ahead(k))

    def rank_copy(k):
        return push(rank_all.at[me], rank_all.at[me], r_s.at[k], r_r.at[me], ahead(k))

    def part_copy(k):
        return push(part_out.at[behind(k)], part_in.at[me], p_s.at[k], p_r.at[me], behind(k))

    def arrive(ref, recv, at):
        push(ref.at[at], ref.at[at], recv.at[at], recv.at[at], ahead(1)).wait_recv()

    others(lambda k: span_copy(k).start())
    bits = []
    m = n // 2
    while m:
        bits.append(m)
        m //= 2

    def a_copy(m, i):
        slot = lax.rem(me, 2 * m) + 2 * m * i
        at = n // (2 * m) - 1 + i
        mate = me + m - 2 * m * lax.rem(me // m, 2)
        return push(a_all.at[slot], a_all.at[slot], a_s.at[at], a_r.at[slot], mate)

    def each(lo, hi, body):
        def step(k, carry):
            body(k)
            return carry
        lax.fori_loop(lo, hi, step, 0)

    begun = 1
    for at, m in enumerate(bits):
        each(0, n // (2 * m), lambda i: a_copy(m, i).start())
        until = 1 + (n - 1) * (at + 1) // len(bits)
        each(begun, until, lambda k: g_copy(k).start())
        begun = until
        mate = me + m - 2 * m * lax.rem(me // m, 2)
        each(0, n // (2 * m), lambda i: arrive(a_all, a_r, lax.rem(mate, 2 * m) + 2 * m * i))

    t_cols[me] = tok[:, tok_cols(me)]

    acc[...] = jnp.zeros_like(acc)

    def code_step(s):
        acc[...] += dot(tok[:, tok_cols(s)], a_all[s], NN)
    each(0, n, code_step)
    code_all[me] = fold(me, acc[...]).astype(BF16)
    others(lambda k: code_copy(k).start())
    others(lambda k: arrive(s_all, s_r, behind(k)))

    def part_step(k):
        src = behind(k)
        arrive(g_cols, g_r, src)
        part_out[src] = fold(src, dot(g_cols[src], up[...], NT)).astype(BF16)
        part_copy(k).start()
        t_copy(k).start()
    others(part_step)
    own.wait()
    total0 = fold(me, dot(g_cols[me], up[...], NT))
    acc[:half, :128] = total0

    def sum_step(k):
        arrive(part_in, p_r, behind(k))
        acc[:half, :128] += part_in[behind(k)].astype(F32)
    others(sum_step)
    rank_all[me] = (ADAPTER_SCALE * acc[:half, :128]).astype(BF16)
    others(lambda k: rank_copy(k).start())

    wide = widen(me, rank_all[me])

    def gt_step(s):
        gt_out[:, tok_cols(s)] = dot(wide, a_all[s], NT).astype(BF16)
    each(0, n, gt_step)

    others(lambda k: arrive(code_all, c_r, behind(k)))
    ug_out[...] = jnp.zeros_like(ug_out)

    def ug_step(b):
        w = jnp.concatenate([widen(2 * b, code_all[2 * b]), widen(2 * b + 1, code_all[2 * b + 1])], axis=0)
        g = g_cols[pl.ds(2 * b, 2)].reshape(2 * rows, c_cols)
        ug_out[...] += dot(w, g, TN)
    each(0, n // 2, ug_step)

    others(lambda k: arrive(rank_all, r_r, behind(k)))
    others(lambda k: arrive(t_cols, t_r, behind(k)))
    dg_out[...] = jnp.zeros_like(dg_out)

    def dg_step(b):
        w = jnp.concatenate([widen(2 * b, rank_all[2 * b]), widen(2 * b + 1, rank_all[2 * b + 1])], axis=0)
        t = t_cols[pl.ds(2 * b, 2)].reshape(2 * rows, d_cols)
        dg_out[...] += dot(t, w, TN)
    each(0, n // 2, dg_step)

    for m in bits:
        each(0, n // (2 * m), lambda i: a_copy(m, i).wait_send())

    def drain(k):
        for make in (span_copy, g_copy, t_copy, code_copy, part_copy, rank_copy):
            make(k).wait_send()
    others(drain)


def local(tokens, output_gradient, down_factor, up_factor, counts):
    rows, features = tokens.shape
    hidden = output_gradient.shape[1]
    n = lax.axis_size("dp")
    jobs, d_cols, rank = down_factor.shape
    c_cols = up_factor.shape[2]
    wide = jobs * rank
    ends = jnp.cumsum(counts[0])
    starts = ends - counts[0]
    spans = jnp.repeat(jnp.concatenate([starts, ends]).astype(jnp.int32), rank).reshape(jobs, 2 * rank)
    down = down_factor.transpose(1, 0, 2).reshape(d_cols, wide)
    up = up_factor.reshape(wide, c_cols)
    split = c_cols % 128 != 0
    if split:
        output_gradient = output_gradient.reshape(rows, n, c_cols).transpose(1, 0, 2)
    vmem = pl.BlockSpec(memory_space=pltpu.VMEM)
    sems = pltpu.SemaphoreType.DMA((n,))
    packed = (n, rows // 2, 2 * rank)
    gt, dg, ug = pl.pallas_call(
        functools.partial(kernel, n, split),
        out_shape=(
            jax.ShapeDtypeStruct((rows, features), BF16),
            jax.ShapeDtypeStruct((d_cols, wide), F32),
            jax.ShapeDtypeStruct((wide, c_cols), F32),
        ),
        in_specs=[vmem, pl.BlockSpec(memory_space=pl.ANY), vmem, vmem, vmem],
        out_specs=(vmem, vmem, vmem),
        scratch_shapes=[
            pltpu.VMEM((n, rows, c_cols), BF16),
            pltpu.VMEM((n, rows, d_cols), BF16),
            pltpu.VMEM((n, d_cols, wide), BF16),
            pltpu.VMEM((n, jobs, 2 * rank), jnp.int32),
            pltpu.VMEM(packed, BF16),
            pltpu.VMEM(packed, BF16),
            pltpu.VMEM(packed, BF16),
            pltpu.VMEM(packed, BF16),
            pltpu.VMEM((rows, wide), F32),
            pltpu.SemaphoreType.DMA,
        ] + [sems] * 14,
        compiler_params=pltpu.CompilerParams(
            collective_id=0, has_side_effects=True, vmem_limit_bytes=56 * 1024 * 1024
        ),
    )(tokens, output_gradient, down, up, spans)
    down_grad = dg.reshape(d_cols, jobs, rank).transpose(1, 0, 2)
    up_grad = (ADAPTER_SCALE * ug).reshape(jobs, rank, c_cols)
    return gt, down_grad, up_grad


def solution(mesh):
    return jax.shard_map(
        local,
        mesh=mesh,
        in_specs=(
            P(("groups", "dp"), None),
            P(("groups", "dp"), None),
            P("groups", "dp", None),
            P("groups", None, "dp"),
            P(("groups", "dp"), None),
        ),
        out_specs=(P(("groups", "dp"), None), P("groups", "dp", None), P("groups", None, "dp")),
        check_vma=False,
    )
```

```python
import functools

import jax
import jax.numpy as jnp
from jax import lax
from jax.experimental import pallas as pl
from jax.experimental.pallas import tpu as pltpu
from jax.sharding import PartitionSpec as P

ADAPTER_SCALE = 2.0
MESH = pl.DeviceIdType.MESH
F32 = jnp.float32
BF16 = jnp.bfloat16
NN = (((1,), (0,)), ((), ()))
NT = (((1,), (1,)), ((), ()))
TN = (((0,), (0,)), ((), ()))


def dot(a, b, dims):
    return lax.dot_general(a, b, dims, preferred_element_type=F32)


def kernel(
    n, split, tok, grad, down, up, counts, gt_out, dg_out, ug_out,
    g_cols, t_cols, a_all, s_all, code_all, rank_all, part_out, part_in, acc,
    own_sem, g_s, g_r, t_s, t_r, a_s, a_r, s_s, s_r, c_s, c_r, p_s, p_r, r_s, r_r,
):
    me = lax.axis_index("dp")
    rows = tok.shape[0]
    half = rows // 2
    d_cols = t_cols.shape[2]
    c_cols = g_cols.shape[2]
    pairs = s_all.shape[1] // 2

    def push(src, dst, send, recv, to):
        return pltpu.make_async_remote_copy(
            src_ref=src, dst_ref=dst, send_sem=send, recv_sem=recv,
            device_id={"dp": to}, device_id_type=MESH,
        )

    def others(body):
        def step(k, carry):
            body(k)
            return carry
        lax.fori_loop(1, n, step, 0)

    def flip(a, b):
        total, bit = 0, 1
        while bit < n:
            total += lax.rem(a // bit + b // bit, 2) * bit
            bit *= 2
        return total

    def ahead(k):
        i = k - 1
        odd = lax.rem(i, 2)
        side = lax.rem(me, 2)
        far = lax.rem(odd + side + 1, 2)
        return flip(me, far * (n // 2) + (i + odd) // 2 + side * (1 - odd))

    behind = ahead

    def grad_slice(at):
        if split:
            return grad.at[at]
        return grad.at[:, pl.ds(pl.multiple_of(at * c_cols, 128), c_cols)]

    def tok_cols(at):
        return pl.ds(pl.multiple_of(at * d_cols, 128), d_cols)

    lane = lax.broadcasted_iota(jnp.int32, (half, 128), 1)
    place = lax.broadcasted_iota(jnp.int32, (rows, 128), 0)

    def mask(block, p):
        return (place >= s_all[block, p : p + 1, :]) & (place < s_all[block, pairs + p : pairs + p + 1, :])

    def fold(block, terms):
        total = jnp.zeros((rows, 128), F32)
        for p in range(pairs):
            total += jnp.where(mask(block, p), terms[:, 128 * p : 128 * (p + 1)], 0.0)
        twice = total + pltpu.roll(total, 64, 1)
        return jnp.where(lane < 64, twice[:half], twice[half:])

    def widen(block, packed):
        x = packed.astype(F32)
        y = pltpu.roll(x, 64, 1)
        both = jnp.concatenate([jnp.where(lane < 64, x, y), jnp.where(lane < 64, y, x)], axis=0)
        return jnp.concatenate([jnp.where(mask(block, p), both, 0.0) for p in range(pairs)], axis=1).astype(BF16)

    other = lax.rem(me + 1, n)
    barrier = pltpu.get_barrier_semaphore()
    others(lambda k: pl.semaphore_signal(barrier, inc=1, device_id={"dp": ahead(k)}, device_id_type=MESH))
    row = lax.broadcasted_iota(jnp.int32, (2 * pairs, 128), 0)
    side = lax.broadcasted_iota(jnp.int32, (2 * pairs, 128), 1) // 64
    spans = jnp.zeros((2 * pairs, 128), jnp.int32)
    at = jnp.int32(0)
    for j in range(2 * pairs):
        spans = jnp.where((row == j // 2) & (side == j % 2), at, spans)
        at = at + counts[0, j]
        spans = jnp.where((row == pairs + j // 2) & (side == j % 2), at, spans)
    s_all[me] = spans
    a_all[me] = down[...]
    own = pltpu.make_async_copy(grad_slice(me), g_cols.at[me], own_sem)
    own.start()
    pl.semaphore_wait(barrier, n - 1)

    def span_copy(k):
        return push(s_all.at[me], s_all.at[me], s_s.at[k], s_r.at[me], ahead(k))

    def g_copy(k):
        return push(grad_slice(ahead(k)), g_cols.at[me], g_s.at[k], g_r.at[me], ahead(k))

    def t_copy(k):
        return push(tok.at[:, tok_cols(ahead(k))], t_cols.at[me], t_s.at[k], t_r.at[me], ahead(k))

    def code_copy(k):
        return push(code_all.at[me], code_all.at[me], c_s.at[k], c_r.at[me], ahead(k))

    def rank_copy(k):
        return push(rank_all.at[me], rank_all.at[me], r_s.at[k], r_r.at[me], ahead(k))

    def part_copy(k):
        return push(part_out.at[behind(k)], part_in.at[me], p_s.at[k], p_r.at[me], behind(k))

    def arrive(ref, recv, at):
        push(ref.at[at], ref.at[at], recv.at[at], recv.at[at], other).wait_recv()

    others(lambda k: span_copy(k).start())
    bits = []
    m = n // 2
    while m:
        bits.append(m)
        m //= 2

    def a_copy(m, i):
        slot = lax.rem(me, 2 * m) + 2 * m * i
        at = n // (2 * m) - 1 + i
        mate = me + m - 2 * m * lax.rem(me // m, 2)
        return push(a_all.at[slot], a_all.at[slot], a_s.at[at], a_r.at[slot], mate)

    def each(lo, hi, body):
        def step(k, carry):
            body(k)
            return carry
        lax.fori_loop(lo, hi, step, 0)

    begun = 1
    for at, m in enumerate(bits):
        each(0, n // (2 * m), lambda i: a_copy(m, i).start())
        until = 1 + min(n - 1, (n - 1) * (at + 1) // max(1, len(bits) - 1))
        each(begun, until, lambda k: g_copy(k).start())
        begun = until
        mate = me + m - 2 * m * lax.rem(me // m, 2)
        each(0, n // (2 * m), lambda i: arrive(a_all, a_r, lax.rem(mate, 2 * m) + 2 * m * i))

    t_cols[me] = tok[:, tok_cols(me)]

    acc[...] = jnp.zeros_like(acc)

    def code_step(s):
        acc[...] += dot(tok[:, tok_cols(s)], a_all[s], NT)
    each(0, n, code_step)
    code_all[me] = fold(me, acc[...]).astype(BF16)
    others(lambda k: code_copy(k).start())
    others(lambda k: arrive(s_all, s_r, behind(k)))

    def part_step(k):
        src = behind(k)
        arrive(g_cols, g_r, src)
        part_out[src] = fold(src, dot(g_cols[src], up[...], NT)).astype(BF16)
        part_copy(k).start()
        t_copy(k).start()
    others(part_step)
    own.wait()
    total0 = fold(me, dot(g_cols[me], up[...], NT))
    acc[:half, :128] = total0

    def sum_step(k):
        arrive(part_in, p_r, behind(k))
        acc[:half, :128] += part_in[behind(k)].astype(F32)
    others(sum_step)
    rank_all[me] = (ADAPTER_SCALE * acc[:half, :128]).astype(BF16)
    others(lambda k: rank_copy(k).start())

    wide = widen(me, rank_all[me])

    def gt_step(s):
        gt_out[:, tok_cols(s)] = dot(wide, a_all[s], NN).astype(BF16)
    each(0, n, gt_step)

    others(lambda k: arrive(code_all, c_r, behind(k)))
    ug_out[...] = jnp.zeros_like(ug_out)

    def ug_step(b):
        w = jnp.concatenate([widen(2 * b, code_all[2 * b]), widen(2 * b + 1, code_all[2 * b + 1])], axis=0)
        g = g_cols[pl.ds(2 * b, 2)].reshape(2 * rows, c_cols)
        ug_out[...] += dot(w, g, TN)
    each(0, n // 2, ug_step)

    others(lambda k: arrive(rank_all, r_r, behind(k)))
    others(lambda k: arrive(t_cols, t_r, behind(k)))
    dg_out[...] = jnp.zeros_like(dg_out)

    def dg_step(b):
        w = jnp.concatenate([widen(2 * b, rank_all[2 * b]), widen(2 * b + 1, rank_all[2 * b + 1])], axis=0)
        t = t_cols[pl.ds(2 * b, 2)].reshape(2 * rows, d_cols)
        dg_out[...] += dot(w, t, TN)
    each(0, n // 2, dg_step)

    for m in bits:
        each(0, n // (2 * m), lambda i: a_copy(m, i).wait_send())

    def drain(k):
        for make in (span_copy, g_copy, t_copy, code_copy, part_copy, rank_copy):
            make(k).wait_send()
    others(drain)


def local(tokens, output_gradient, down_factor, up_factor, counts):
    rows, features = tokens.shape
    hidden = output_gradient.shape[1]
    n = lax.axis_size("dp")
    jobs, d_cols, rank = down_factor.shape
    c_cols = up_factor.shape[2]
    wide = jobs * rank
    down = down_factor.transpose(0, 2, 1).reshape(wide, d_cols)
    up = up_factor.reshape(wide, c_cols)
    split = c_cols % 128 != 0
    if split:
        output_gradient = output_gradient.reshape(rows, n, c_cols).transpose(1, 0, 2)
    vmem = pl.BlockSpec(memory_space=pltpu.VMEM)
    sems = pltpu.SemaphoreType.DMA((n,))
    packed = (n, rows // 2, 2 * rank)
    gt, dg, ug = pl.pallas_call(
        functools.partial(kernel, n, split),
        out_shape=(
            jax.ShapeDtypeStruct((rows, features), BF16),
            jax.ShapeDtypeStruct((wide, d_cols), F32),
            jax.ShapeDtypeStruct((wide, c_cols), F32),
        ),
        in_specs=[vmem, pl.BlockSpec(memory_space=pl.ANY), vmem, vmem, pl.BlockSpec(memory_space=pltpu.SMEM)],
        out_specs=(vmem, vmem, vmem),
        scratch_shapes=[
            pltpu.VMEM((n, rows, c_cols), BF16),
            pltpu.VMEM((n, rows, d_cols), BF16),
            pltpu.VMEM((n, wide, d_cols), BF16),
            pltpu.VMEM((n, jobs, 2 * rank), jnp.int32),
            pltpu.VMEM(packed, BF16),
            pltpu.VMEM(packed, BF16),
            pltpu.VMEM(packed, BF16),
            pltpu.VMEM(packed, BF16),
            pltpu.VMEM((rows, wide), F32),
            pltpu.SemaphoreType.DMA,
        ] + [sems] * 14,
        compiler_params=pltpu.CompilerParams(
            collective_id=0, has_side_effects=True, vmem_limit_bytes=56 * 1024 * 1024
        ),
    )(tokens, output_gradient, down, up, counts)
    down_grad = dg.reshape(jobs, rank, d_cols).transpose(0, 2, 1)
    up_grad = (ADAPTER_SCALE * ug).reshape(jobs, rank, c_cols)
    return gt, down_grad, up_grad


def solution(mesh):
    return jax.shard_map(
        local,
        mesh=mesh,
        in_specs=(
            P(("groups", "dp"), None),
            P(("groups", "dp"), None),
            P("groups", "dp", None),
            P("groups", None, "dp"),
            P(("groups", "dp"), None),
        ),
        out_specs=(P(("groups", "dp"), None), P("groups", "dp", None), P("groups", None, "dp")),
        check_vma=False,
    )
```

```python
import functools

import jax
import jax.numpy as jnp
from jax import lax
from jax.experimental import pallas as pl
from jax.experimental.pallas import tpu as pltpu
from jax.sharding import PartitionSpec as P

ADAPTER_SCALE = 2.0
MESH = pl.DeviceIdType.MESH
F32 = jnp.float32
BF16 = jnp.bfloat16
NN = (((1,), (0,)), ((), ()))
NT = (((1,), (1,)), ((), ()))
TN = (((0,), (0,)), ((), ()))


def dot(a, b, dims):
    return lax.dot_general(a, b, dims, preferred_element_type=F32)


def kernel(
    n, split, tok, grad, down, up, counts, gt_out, dg_out, ug_out,
    g_cols, t_cols, a_all, s_all, code_all, rank_all, part_out, part_in, acc,
    own_sem, g_s, g_r, t_s, t_r, a_s, a_r, s_s, s_r, c_s, c_r, p_s, p_r, r_s, r_r,
):
    me = lax.axis_index("dp")
    rows = tok.shape[0]
    half = rows // 2
    d_cols = t_cols.shape[2]
    c_cols = g_cols.shape[2]
    pairs = s_all.shape[1] // 2

    def push(src, dst, send, recv, to):
        return pltpu.make_async_remote_copy(
            src_ref=src, dst_ref=dst, send_sem=send, recv_sem=recv,
            device_id={"dp": to}, device_id_type=MESH,
        )

    def others(body):
        def step(k, carry):
            body(k)
            return carry
        lax.fori_loop(1, n, step, 0)

    def flip(a, b):
        total, bit = 0, 1
        while bit < n:
            total += lax.rem(a // bit + b // bit, 2) * bit
            bit *= 2
        return total

    def ahead(k):
        i = k - 1
        odd = lax.rem(i, 2)
        side = lax.rem(me, 2)
        far = lax.rem(odd + side + 1, 2)
        return flip(me, far * (n // 2) + (i + odd) // 2 + side * (1 - odd))

    behind = ahead

    def grad_slice(at):
        if split:
            return grad.at[at]
        return grad.at[:, pl.ds(pl.multiple_of(at * c_cols, 128), c_cols)]

    def tok_cols(at):
        return pl.ds(pl.multiple_of(at * d_cols, 128), d_cols)

    lane = lax.broadcasted_iota(jnp.int32, (half, 128), 1)
    place = lax.broadcasted_iota(jnp.int32, (rows, 128), 0)

    def mask(block, p):
        return (place >= s_all[block, p : p + 1, :]) & (place < s_all[block, pairs + p : pairs + p + 1, :])

    def fold(block, terms):
        total = jnp.zeros((rows, 128), F32)
        for p in range(pairs):
            total += jnp.where(mask(block, p), terms[:, 128 * p : 128 * (p + 1)], 0.0)
        twice = total + pltpu.roll(total, 64, 1)
        return jnp.where(lane < 64, twice[:half], twice[half:])

    def widen(block, packed):
        x = packed.astype(F32)
        y = pltpu.roll(x, 64, 1)
        both = jnp.concatenate([jnp.where(lane < 64, x, y), jnp.where(lane < 64, y, x)], axis=0)
        return jnp.concatenate([jnp.where(mask(block, p), both, 0.0) for p in range(pairs)], axis=1).astype(BF16)

    other = lax.rem(me + 1, n)
    barrier = pltpu.get_barrier_semaphore()
    others(lambda k: pl.semaphore_signal(barrier, inc=1, device_id={"dp": ahead(k)}, device_id_type=MESH))
    row = lax.broadcasted_iota(jnp.int32, (2 * pairs, 128), 0)
    side = lax.broadcasted_iota(jnp.int32, (2 * pairs, 128), 1) // 64
    spans = jnp.zeros((2 * pairs, 128), jnp.int32)
    at = jnp.int32(0)
    for j in range(2 * pairs):
        spans = jnp.where((row == j // 2) & (side == j % 2), at, spans)
        at = at + counts[0, j]
        spans = jnp.where((row == pairs + j // 2) & (side == j % 2), at, spans)
    s_all[me] = spans
    a_all[me] = down[...]
    own = pltpu.make_async_copy(grad_slice(me), g_cols.at[me], own_sem)
    own.start()
    pl.semaphore_wait(barrier, n - 1)

    def span_copy(k):
        return push(s_all.at[me], s_all.at[me], s_s.at[k], s_r.at[me], ahead(k))

    def g_copy(k):
        return push(grad_slice(ahead(k)), g_cols.at[me], g_s.at[k], g_r.at[me], ahead(k))

    def t_copy(k):
        return push(tok.at[:, tok_cols(ahead(k))], t_cols.at[me], t_s.at[k], t_r.at[me], ahead(k))

    def code_copy(k):
        return push(code_all.at[me], code_all.at[me], c_s.at[k], c_r.at[me], ahead(k))

    def rank_copy(k):
        return push(rank_all.at[me], rank_all.at[me], r_s.at[k], r_r.at[me], ahead(k))

    def part_copy(k):
        return push(part_out.at[behind(k)], part_in.at[me], p_s.at[k], p_r.at[me], behind(k))

    def arrive(ref, recv, at):
        push(ref.at[at], ref.at[at], recv.at[at], recv.at[at], other).wait_recv()

    others(lambda k: span_copy(k).start())
    bits = []
    m = n // 2
    while m:
        bits.append(m)
        m //= 2

    def a_copy(m, i):
        slot = lax.rem(me, 2 * m) + 2 * m * i
        at = n // (2 * m) - 1 + i
        mate = me + m - 2 * m * lax.rem(me // m, 2)
        return push(a_all.at[slot], a_all.at[slot], a_s.at[at], a_r.at[slot], mate)

    def each(lo, hi, body):
        def step(k, carry):
            body(k)
            return carry
        lax.fori_loop(lo, hi, step, 0)

    begun = 1
    for at, m in enumerate(bits):
        each(0, n // (2 * m), lambda i: a_copy(m, i).start())
        until = 1 + min(n - 1, (n - 1) * (at + 1) // max(1, len(bits) - 1))
        each(begun, until, lambda k: g_copy(k).start())
        begun = until
        mate = me + m - 2 * m * lax.rem(me // m, 2)
        each(0, n // (2 * m), lambda i: arrive(a_all, a_r, lax.rem(mate, 2 * m) + 2 * m * i))

    t_cols[me] = tok[:, tok_cols(me)]

    acc[...] = jnp.zeros_like(acc)

    def code_step(s):
        acc[...] += dot(tok[:, tok_cols(s)], a_all[s], NT)
    each(0, n, code_step)
    code_all[me] = fold(me, acc[...]).astype(BF16)
    others(lambda k: code_copy(k).start())
    others(lambda k: arrive(s_all, s_r, behind(k)))

    def part_step(k):
        src = behind(k)
        arrive(g_cols, g_r, src)
        part_out[src] = fold(src, dot(g_cols[src], up[...], NT)).astype(BF16)
        part_copy(k).start()

    def both_step(k):
        part_step(k)
        t_copy(k).start()
    soon, later = n * 8 // 16, n * 12 // 16
    each(1, soon, both_step)
    each(soon, n, part_step)
    each(soon, later, lambda k: t_copy(k).start())
    own.wait()
    total0 = fold(me, dot(g_cols[me], up[...], NT))
    acc[:half, :128] = total0

    def sum_step(k):
        arrive(part_in, p_r, behind(k))
        acc[:half, :128] += part_in[behind(k)].astype(F32)
    others(sum_step)
    rank_all[me] = (ADAPTER_SCALE * acc[:half, :128]).astype(BF16)
    others(lambda k: rank_copy(k).start())
    each(later, n, lambda k: t_copy(k).start())

    wide = widen(me, rank_all[me])

    def gt_step(s):
        gt_out[:, tok_cols(s)] = dot(wide, a_all[s], NN).astype(BF16)
    each(0, n, gt_step)

    others(lambda k: arrive(code_all, c_r, behind(k)))
    ug_out[...] = jnp.zeros_like(ug_out)

    def ug_step(b):
        w = jnp.concatenate([widen(2 * b, code_all[2 * b]), widen(2 * b + 1, code_all[2 * b + 1])], axis=0)
        g = g_cols[pl.ds(2 * b, 2)].reshape(2 * rows, c_cols)
        ug_out[...] += dot(w, g, TN)
    each(0, n // 2, ug_step)

    others(lambda k: arrive(rank_all, r_r, behind(k)))
    others(lambda k: arrive(t_cols, t_r, behind(k)))
    dg_out[...] = jnp.zeros_like(dg_out)

    def dg_step(b):
        w = jnp.concatenate([widen(2 * b, rank_all[2 * b]), widen(2 * b + 1, rank_all[2 * b + 1])], axis=0)
        t = t_cols[pl.ds(2 * b, 2)].reshape(2 * rows, d_cols)
        dg_out[...] += dot(w, t, TN)
    each(0, n // 2, dg_step)

    for m in bits:
        each(0, n // (2 * m), lambda i: a_copy(m, i).wait_send())

    def drain(k):
        for make in (span_copy, g_copy, t_copy, code_copy, part_copy, rank_copy):
            make(k).wait_send()
    others(drain)


def local(tokens, output_gradient, down_factor, up_factor, counts):
    rows, features = tokens.shape
    hidden = output_gradient.shape[1]
    n = lax.axis_size("dp")
    jobs, d_cols, rank = down_factor.shape
    c_cols = up_factor.shape[2]
    wide = jobs * rank
    down = down_factor.transpose(0, 2, 1).reshape(wide, d_cols)
    up = up_factor.reshape(wide, c_cols)
    split = c_cols % 128 != 0
    if split:
        output_gradient = output_gradient.reshape(rows, n, c_cols).transpose(1, 0, 2)
    vmem = pl.BlockSpec(memory_space=pltpu.VMEM)
    sems = pltpu.SemaphoreType.DMA((n,))
    packed = (n, rows // 2, 2 * rank)
    gt, dg, ug = pl.pallas_call(
        functools.partial(kernel, n, split),
        out_shape=(
            jax.ShapeDtypeStruct((rows, features), BF16),
            jax.ShapeDtypeStruct((wide, d_cols), F32),
            jax.ShapeDtypeStruct((wide, c_cols), F32),
        ),
        in_specs=[vmem, pl.BlockSpec(memory_space=pl.ANY), vmem, vmem, pl.BlockSpec(memory_space=pltpu.SMEM)],
        out_specs=(vmem, vmem, vmem),
        scratch_shapes=[
            pltpu.VMEM((n, rows, c_cols), BF16),
            pltpu.VMEM((n, rows, d_cols), BF16),
            pltpu.VMEM((n, wide, d_cols), BF16),
            pltpu.VMEM((n, jobs, 2 * rank), jnp.int32),
            pltpu.VMEM(packed, BF16),
            pltpu.VMEM(packed, BF16),
            pltpu.VMEM(packed, BF16),
            pltpu.VMEM(packed, BF16),
            pltpu.VMEM((rows, wide), F32),
            pltpu.SemaphoreType.DMA,
        ] + [sems] * 14,
        compiler_params=pltpu.CompilerParams(
            collective_id=0, has_side_effects=True, vmem_limit_bytes=56 * 1024 * 1024
        ),
    )(tokens, output_gradient, down, up, counts)
    down_grad = dg.reshape(jobs, rank, d_cols).transpose(0, 2, 1)
    up_grad = (ADAPTER_SCALE * ug).reshape(jobs, rank, c_cols)
    return gt, down_grad, up_grad


def solution(mesh):
    return jax.shard_map(
        local,
        mesh=mesh,
        in_specs=(
            P(("groups", "dp"), None),
            P(("groups", "dp"), None),
            P("groups", "dp", None),
            P("groups", None, "dp"),
            P(("groups", "dp"), None),
        ),
        out_specs=(P(("groups", "dp"), None), P("groups", "dp", None), P("groups", None, "dp")),
        check_vma=False,
    )
```
